32 devices in a mesh: groups: 2 (over x), rows: 8 (over z, y), chan: 2 (over core).
Axes of the slice: x: 2, y: 2, z: 4, core: 2. Of those that a mesh axis runs over, the one named last changes fastest.
Arguments:
- pair: bfloat16 [768, 384, 128], P(('groups', 'rows')), parts along dimension 0, may hold values from -6 to 6
- seq_len: int32 [2], P('groups'), parts along dimension 0, may hold values from 192 to 384
- pair_mask: int32 [768, 384], P(('groups', 'rows')), parts along dimension 0, may hold values 0 or 1
- ln_in_gain: bfloat16 [2, 128], replicated, may hold values from 0.25 to 1.75
- w_proj: bfloat16 [2, 4, 128, 64], P(None, None, None, 'chan'), may hold values from -0.5 to 0.5
- w_gate: bfloat16 [2, 128, 128], replicated, may hold values from -0.5 to 0.5
- ln_out_gain: bfloat16 [2, 64], P(None, 'chan'), may hold values from 0.25 to 1.75
- w_out: bfloat16 [2, 64, 128], P(None, 'chan'), may hold values from -0.75 to 0.75
Outputs:
- pair_out: bfloat16 [768, 384, 128], P(('groups', 'rows', 'chan')), parts along dimension 0
The draws below stay inside these ranges and needn't reach their ends.
There are 2 independent parts, one for each index of `groups`. The reference program is written for one: setup_inputs(seed, part) draws one part's arguments, and reference() takes and returns one part's arrays. A program takes and returns all parts, laid end to end along the dimension named above; an argument that names none is the same for every part. Nothing has to cross between parts.
Inputs may be any that keep to these rules, and one draw needn't show every extreme that they name: Tokens at and after seq_len are padding.
All inputs are finite; a program needn't handle non-finite values. No bound on the sum of `pair_mask` on one device may be relied on, other than what follows from the above.
Results may differ from the reference program's by a relative error of at most 0.008.
Values may be sent and summed in bfloat16 or wider, within the bound.
A program may use at most 128 MiB of HBM per device.

```python
import jax
import jax.numpy as jnp
from jax import lax

C = 128
CH = 64
NTOK = 384


def place_ends(result, rng, low, top_value):
    shape = result.shape
    spot = [jax.random.randint(jax.random.fold_in(rng, axis), (), 0, shape[axis]) for axis in range(len(shape))]
    result = result.at[tuple(spot)].set(low)
    longest = shape.index(max(shape))
    spot[longest] = (spot[longest] + 1) % shape[longest]
    return result.at[tuple(spot)].set(top_value)


def shard_levels(rng, shape, split, low, high):
    loudness = 1.0
    for axis_at, shards_of in split:
        draws = jax.random.uniform(jax.random.fold_in(jax.random.fold_in(rng, 6), axis_at), (shards_of,), jnp.float32, low / len(split), high / len(split))
        loudness = loudness * jnp.repeat(jnp.exp(draws), shape[axis_at] // shards_of).reshape((-1,) + (1,) * (len(shape) - 1 - axis_at))
    return loudness


def gaussian(stream_key, dims, width, bound, split=(), kind=jnp.bfloat16):
    values = width * jax.random.normal(stream_key, dims, jnp.float32)
    if split:
        values = values * shard_levels(stream_key, dims, split, -0.22, 0.18)
    return jnp.clip(values, -bound, bound).astype(kind)


def setup_inputs(seed: int = 0, part: int = 0) -> dict:
    key_list = jax.random.split(jax.random.key(seed), 9)
    part_splits = jax.random.split(jax.random.fold_in(key_list[8], part), 9)
    pair = gaussian(part_splits[0], (NTOK, NTOK, C), 1.0, 6.0, ((0, 8),))
    seq_len = jax.random.randint(part_splits[1], (1,), NTOK // 2, NTOK + 1).astype(jnp.int32)
    pair_mask = place_ends((jax.random.randint(part_splits[2], (NTOK, NTOK), 0, 10) < 9).astype(jnp.int32), jax.random.fold_in(part_splits[2], 1), 0, 1)
    ln_in_gain = jnp.clip(1.0 + 0.15 * jax.random.normal(key_list[3], (2, C), jnp.float32), 0.25, 1.75).astype(jnp.bfloat16)
    w_proj = gaussian(key_list[4], (2, 4, C, CH), C ** -0.5, 0.5, ((3, 2),))
    w_gate = gaussian(key_list[5], (2, C, C), C ** -0.5, 0.5)
    ln_out_gain = jnp.clip(1.0 + 0.15 * jax.random.normal(key_list[6], (2, CH), jnp.float32), 0.25, 1.75).astype(jnp.bfloat16)
    w_out = gaussian(key_list[7], (2, CH, C), CH ** -0.5, 0.75, ((1, 2),))
    return dict(pair=pair, seq_len=seq_len, pair_mask=pair_mask, ln_in_gain=ln_in_gain, w_proj=w_proj, w_gate=w_gate, ln_out_gain=ln_out_gain, w_out=w_out)


def normalize(values, gain_row):
    average = lax.optimization_barrier(jnp.mean(values, axis=-1, keepdims=True))
    squares_mean = lax.optimization_barrier(jnp.mean(values * values, axis=-1, keepdims=True))
    spread = jnp.maximum(squares_mean - average * average, 0.0)
    return (values - average) * lax.rsqrt(spread + 1e-05) * gain_row

def reference(pair, seq_len, pair_mask, ln_in_gain, w_proj, w_gate, ln_out_gain, w_out):
    valid = (jnp.arange(NTOK) < seq_len[0]).astype(jnp.float32)
    pair_weight = pair_mask.astype(jnp.float32) * valid[:, None] * valid[None, :]
    current = pair
    for layer_index in range(2):
        normed = normalize(current.astype(jnp.float32), ln_in_gain[layer_index].astype(jnp.float32)).astype(jnp.bfloat16)
        flattened = normed.reshape(NTOK * NTOK, C)
        projected = [jnp.dot(flattened, w_proj[layer_index, which], preferred_element_type=jnp.float32).reshape(NTOK, NTOK, CH) for which in range(4)]
        left_side = (pair_weight[:, :, None] * jax.nn.sigmoid(projected[0]) * projected[1]).astype(jnp.bfloat16).astype(jnp.float32)
        right_side = (pair_weight[:, :, None] * jax.nn.sigmoid(projected[2]) * projected[3]).astype(jnp.bfloat16).astype(jnp.float32)
        if layer_index == 0:
            product = jnp.einsum('ikc,jkc->ijc', left_side, right_side, precision=lax.Precision.HIGHEST)
        else:
            product = jnp.einsum('kic,kjc->ijc', left_side, right_side, precision=lax.Precision.HIGHEST)
        product = product.astype(jnp.bfloat16)
        scaled = normalize(product.astype(jnp.float32), ln_out_gain[layer_index].astype(jnp.float32)).astype(jnp.bfloat16)
        update = jnp.dot(scaled.reshape(NTOK * NTOK, CH), w_out[layer_index], preferred_element_type=jnp.float32)
        gate_values = jax.nn.sigmoid(jnp.dot(flattened, w_gate[layer_index], preferred_element_type=jnp.float32))
        current = (current.astype(jnp.float32) + (gate_values * update).reshape(NTOK, NTOK, C)).astype(jnp.bfloat16)
    return current
```

```python
import functools

import jax
import jax.numpy as jnp
from jax import lax
from jax.experimental import pallas as pl
from jax.experimental.pallas import tpu as pltpu
from jax.sharding import PartitionSpec as P

F32 = jnp.float32
BF16 = jnp.bfloat16
NT = (((1,), (1,)), ((), ()))
TN = (((0,), (0,)), ((), ()))


def kernel(
    dims, pair_ref, weight_ref, pack_ref, gain_ref, gate_ref, out_ref,
    z, x, wfull, rows_f, left_f, right_f, prod_f, norm_f,
    send_lr, recv_lr, send_p, recv_p,
    local_sem, wsend_sem, wrecv_sem, send_sem, recv_sem,
):
    peers, cores, rows, rows_pad, cols, chans, own, feats = dims
    half = chans // cores
    core = lax.axis_index("chan")
    me = lax.axis_index("rows") * cores + core

    def peer_id(p):
        return {"rows": p // cores, "chan": p % cores}

    load = pltpu.make_async_copy(pair_ref.at[pl.ds(core * rows, rows)], z, local_sem.at[0])
    load.start()
    keep = pltpu.make_async_copy(pack_ref, wfull.at[core], local_sem.at[1])
    keep.start()

    barrier = pltpu.get_barrier_semaphore()

    @pl.loop(1, peers)
    def _(s):
        pl.semaphore_signal(
            barrier, inc=1, device_id=peer_id((me + s) % peers), device_id_type=pl.DeviceIdType.MESH
        )

    pl.semaphore_wait(barrier, peers - 1)

    share = pltpu.make_async_remote_copy(
        src_ref=pack_ref, dst_ref=wfull.at[core], send_sem=wsend_sem, recv_sem=wrecv_sem,
        device_id=peer_id(me - core + 1 - core), device_id_type=pl.DeviceIdType.MESH,
    )
    share.start()
    load.wait()
    keep.wait()
    share.wait()

    def exchange(phase, src, dst, p):
        return pltpu.make_async_remote_copy(
            src_ref=src.at[p], dst_ref=dst.at[me],
            send_sem=send_sem.at[phase, p], recv_sem=recv_sem.at[phase, me],
            device_id=peer_id(p), device_id_type=pl.DeviceIdType.MESH,
        )

    def arrived(phase, src, dst, p):
        return pltpu.make_async_remote_copy(
            src_ref=src.at[p], dst_ref=dst.at[p],
            send_sem=send_sem.at[phase, p], recv_sem=recv_sem.at[phase, p],
            device_id=peer_id(p), device_id_type=pl.DeviceIdType.MESH,
        )

    for u in range(2):
        gain_in = gain_ref[pl.ds(u, 1), :].astype(F32)
        to_lr, from_lr = send_lr.at[u], recv_lr.at[u]
        to_p, from_p = send_p.at[u], recv_p.at[u]

        @pl.loop(0, rows)
        def _(i):
            v = z[i].astype(F32)
            average = jnp.mean(v, axis=1, keepdims=True)
            squares = jnp.mean(v * v, axis=1, keepdims=True)
            spread = jnp.maximum(squares - average * average, 0.0)
            xb = ((v - average) * lax.rsqrt(spread + 1e-5) * gain_in).astype(BF16)
            x[i] = xb
            w = weight_ref[i]
            for h in range(cores):
                p_t = lax.dot_general(wfull[h, u, : 4 * half], xb, NT, preferred_element_type=F32)
                for lr in range(2):
                    g = p_t[2 * lr * half : (2 * lr + 1) * half]
                    val = p_t[(2 * lr + 1) * half : (2 * lr + 2) * half]
                    at = pl.multiple_of(i * (2 * chans) + (lr * chans + h * half), 8)
                    piece = w * jax.nn.sigmoid(g) * val
                    for t in range(cols // 128):
                        rows_f[t, pl.ds(at, half), :] = piece[:, t * 128 : (t + 1) * 128]

        def fill(p, target):
            for lr in range(2):
                for c in range(own):
                    for t in range(cols // 128):
                        target[lr, c, :, t * 128 : (t + 1) * 128] = rows_f[
                            t, pl.ds(lr * chans + p * own + c, rows, stride=2 * chans), :
                        ].astype(BF16)

        @pl.loop(1, peers)
        def _(s):
            p = (me + s) % peers
            fill(p, to_lr.at[p])
            exchange(2 * u, to_lr, from_lr, p).start()

        fill(me, from_lr.at[me])

        @pl.loop(1, peers)
        def _(s):
            p = (me + s) % peers
            arrived(2 * u, to_lr, from_lr, p).wait_recv()

        @pl.loop(0, own)
        def _(c):
            for p in range(peers):
                left_f[p * rows : (p + 1) * rows, :] = from_lr[p, 0, c].astype(F32)
                right_f[p * rows : (p + 1) * rows, :] = from_lr[p, 1, c].astype(F32)
            prod_f[...] = lax.dot_general(
                left_f[...].astype(BF16), right_f[...].astype(BF16), NT if u == 0 else TN,
                preferred_element_type=F32,
            )
            for p in range(peers):
                to_p[p, c] = prod_f[p * rows : (p + 1) * rows, :].astype(BF16)

        @pl.loop(1, peers)
        def _(s):
            exchange(2 * u + 1, to_p, from_p, (me + s) % peers).start()

        from_p[me] = to_p[me]

        @pl.loop(1, peers)
        def _(s):
            p = (me + s) % peers
            arrived(2 * u + 1, to_p, from_p, p).wait_recv()

        def add(p, sums):
            total, squares = sums
            for c in range(own):
                v = from_p[p, c].astype(F32)
                total, squares = total + v, squares + v * v
            return total, squares

        zero = jnp.zeros((rows, cols), F32)
        total, squares = lax.fori_loop(0, peers, add, (zero, zero))
        average = total / chans
        scale = lax.rsqrt(jnp.maximum(squares / chans - average * average, 0.0) + 1e-5)

        @pl.loop(0, peers)
        def _(p):
            for c in range(own):
                at = pl.multiple_of((p * own + c) * rows_pad, 8)
                piece = (from_p[p, c].astype(F32) - average) * scale
                for t in range(cols // 128):
                    norm_f[t, pl.ds(at, rows), :] = piece[:, t * 128 : (t + 1) * 128]

        w_out = jnp.concatenate(
            [wfull[h, u, 4 * half : 5 * half] for h in range(cores)], axis=0
        )
        gain_out = jnp.concatenate(
            [wfull[h, u, 5 * half : 6 * half] for h in range(cores)], axis=0
        ).astype(F32)
        w_gate = gate_ref[u]

        @pl.loop(0, rows)
        def _(i):
            scaled = jnp.concatenate(
                [
                    (norm_f[t, pl.ds(i, chans, stride=rows_pad), :] * gain_out).astype(BF16)
                    for t in range(cols // 128)
                ],
                axis=1,
            )
            update = lax.dot_general(scaled, w_out, TN, preferred_element_type=F32)
            gate = jax.nn.sigmoid(jnp.dot(x[i], w_gate, preferred_element_type=F32))
            result = (z[i].astype(F32) + gate * update).astype(BF16)
            if u == 0:
                z[i] = result
            else:
                out_ref[i] = result

    for u in range(2):

        @pl.loop(1, peers)
        def _(s):
            p = (me + s) % peers
            arrived(2 * u, send_lr.at[u], recv_lr.at[u], p).wait_send()
            arrived(2 * u + 1, send_p.at[u], recv_p.at[u], p).wait_send()


def shards(pair, seq_len, pair_mask, ln_in_gain, w_proj, w_gate, ln_out_gain, w_out):
    rows_chip, cols, feats = pair.shape
    cores = lax.axis_size("chan")
    peers = lax.axis_size("rows") * cores
    rows = rows_chip // cores
    rows_pad = -(-rows // 8) * 8
    half = w_proj.shape[3]
    chans = half * cores
    own = chans // peers
    first = (lax.axis_index("rows") * cores + lax.axis_index("chan")) * rows
    valid = (jnp.arange(cols) < seq_len[0]).astype(F32)
    mask = lax.dynamic_slice_in_dim(pair_mask, lax.axis_index("chan") * rows, rows, 0)
    weight = (
        mask.astype(F32) * lax.dynamic_slice_in_dim(valid, first, rows)[:, None] * valid[None, :]
    )[:, None, :]
    pack = jnp.concatenate(
        [
            w_proj.transpose(0, 1, 3, 2).reshape(2, 4 * half, feats),
            w_out,
            jnp.broadcast_to(ln_out_gain[:, :, None], (2, half, feats)),
        ],
        axis=1,
    )
    dims = (peers, cores, rows, rows_pad, cols, chans, own, feats)
    tiles = cols // 128
    vmem = pl.BlockSpec(memory_space=pltpu.VMEM)
    return pl.pallas_call(
        functools.partial(kernel, dims),
        out_shape=jax.ShapeDtypeStruct((rows, cols, feats), BF16),
        in_specs=[pl.BlockSpec(memory_space=pl.ANY), vmem, vmem, vmem, vmem],
        out_specs=vmem,
        scratch_shapes=[
            pltpu.VMEM((rows, cols, feats), BF16),
            pltpu.VMEM((rows, cols, feats), BF16),
            pltpu.VMEM((cores,) + pack.shape, BF16),
            pltpu.VMEM((tiles, rows * 2 * chans, 128), F32),
            pltpu.VMEM((cols, cols), F32),
            pltpu.VMEM((cols, cols), F32),
            pltpu.VMEM((cols, cols), F32),
            pltpu.VMEM((tiles, chans * rows_pad, 128), F32),
            pltpu.VMEM((2, peers, 2, own, rows, cols), BF16),
            pltpu.VMEM((2, peers, 2, own, rows, cols), BF16),
            pltpu.VMEM((2, peers, own, rows, cols), BF16),
            pltpu.VMEM((2, peers, own, rows, cols), BF16),
            pltpu.SemaphoreType.DMA((2,)),
            pltpu.SemaphoreType.DMA,
            pltpu.SemaphoreType.DMA,
            pltpu.SemaphoreType.DMA((4, peers)),
            pltpu.SemaphoreType.DMA((4, peers)),
        ],
        compiler_params=pltpu.CompilerParams(
            collective_id=0, has_side_effects=True, vmem_limit_bytes=60 * 1024 * 1024
        ),
        name="triangle",
    )(pair, weight, pack, ln_in_gain, w_gate)


def solution(mesh):
    in_specs = (
        P(("groups", "rows"), None, None),
        P("groups"),
        P(("groups", "rows"), None),
        P(),
        P(None, None, None, "chan"),
        P(),
        P(None, "chan"),
        P(None, "chan", None),
    )
    out_specs = P(("groups", "rows", "chan"), None, None)
    return jax.shard_map(shards, mesh=mesh, in_specs=in_specs, out_specs=out_specs, check_vma=False)
```

```python
import functools

import jax
import jax.numpy as jnp
from jax import lax
from jax.experimental import pallas as pl
from jax.experimental.pallas import tpu as pltpu
from jax.sharding import PartitionSpec as P

F32 = jnp.float32
BF16 = jnp.bfloat16
NT = (((1,), (1,)), ((), ()))
TN = (((0,), (0,)), ((), ()))


def kernel(
    dims, pair_ref, weight_ref, pack_ref, gain_ref, gate_ref, out_ref,
    z, x, wfull, rows_f, left_f, right_f, prod_f, norm_f,
    send_lr, recv_lr, recv_far, send_p, recv_p, send_q, recv_q,
    local_sem, wsend_sem, wrecv_sem, send_sem, recv_sem,
):
    slots, cores, rows, rows_pad, cols, chans, own, feats = dims
    peers = 2 * slots
    half = chans // cores
    slots_core = slots // cores
    core = lax.axis_index("chan")
    me = lax.axis_index("rows") * cores + core
    side = me // slots
    slot = me % slots

    def device(p):
        return {"rows": p // cores, "chan": p % cores}

    load = pltpu.make_async_copy(pair_ref.at[pl.ds(core * rows, rows)], z, local_sem.at[0])
    load.start()
    keep = pltpu.make_async_copy(pack_ref, wfull.at[core], local_sem.at[1])
    keep.start()

    barrier = pltpu.get_barrier_semaphore()

    @pl.loop(1, peers)
    def _(s):
        pl.semaphore_signal(
            barrier, inc=1, device_id=device((me + s) % peers), device_id_type=pl.DeviceIdType.MESH
        )

    pl.semaphore_wait(barrier, peers - 1)

    share = pltpu.make_async_remote_copy(
        src_ref=pack_ref, dst_ref=wfull.at[core], send_sem=wsend_sem, recv_sem=wrecv_sem,
        device_id=device(me - core + 1 - core), device_id_type=pl.DeviceIdType.MESH,
    )
    share.start()
    load.wait()

    def send(phase, src, dst, far, q):
        return pltpu.make_async_remote_copy(
            src_ref=src, dst_ref=dst.at[slot],
            send_sem=send_sem.at[phase, q], recv_sem=recv_sem.at[phase, slot],
            device_id=device((1 - side if far else side) * slots + q),
            device_id_type=pl.DeviceIdType.MESH,
        )

    def arrival(phase, src, dst, far, q):
        return pltpu.make_async_remote_copy(
            src_ref=src, dst_ref=dst.at[q],
            send_sem=send_sem.at[phase, q], recv_sem=recv_sem.at[phase, q],
            device_id=device((1 - side if far else side) * slots + q),
            device_id_type=pl.DeviceIdType.MESH,
        )

    def normalize_rows(u):
        gain_in = gain_ref[pl.ds(u, 1), :].astype(F32)

        @pl.loop(0, rows)
        def _(i):
            v = z[i].astype(F32)
            average = jnp.mean(v, axis=1, keepdims=True)
            squares = jnp.mean(v * v, axis=1, keepdims=True)
            spread = jnp.maximum(squares - average * average, 0.0)
            x[i] = ((v - average) * lax.rsqrt(spread + 1e-5) * gain_in).astype(BF16)

    def project(u, h):
        @pl.loop(0, rows)
        def _(i):
            w = weight_ref[i]
            p_t = lax.dot_general(wfull[h, u, : 4 * half], x[i], NT, preferred_element_type=F32)
            for lr in range(2):
                g = p_t[2 * lr * half : (2 * lr + 1) * half]
                val = p_t[(2 * lr + 1) * half : (2 * lr + 2) * half]
                at = pl.multiple_of(i * (2 * half) + lr * half, 8)
                piece = w * jax.nn.sigmoid(g) * val
                for t in range(cols // 128):
                    rows_f[t, pl.ds(at, half), :] = piece[:, t * 128 : (t + 1) * 128]

    def fill(q, target):
        for lr in range(2):
            for c in range(own):
                for t in range(cols // 128):
                    target[lr, c, :, t * 128 : (t + 1) * 128] = rows_f[
                        t, pl.ds(lr * half + q * own + c, rows, stride=2 * half), :
                    ].astype(BF16)

    for u in range(2):
        to_lr, from_lr = send_lr.at[u], recv_lr.at[u]
        near = 3 * u
        normalize_rows(u)
        if u == 0:
            keep.wait()
            share.wait()

        for turn in range(cores):
            h = (slot // slots_core + 1 + turn) % cores
            project(u, h)

            @pl.loop(0, slots_core)
            def _(s):
                r = (slot + s) % slots_core
                q = h * slots_core + r
                fill(r, to_lr.at[q])
                if u == 0:
                    send(1, to_lr.at[q, 1], recv_far, True, q).start()

                @pl.when(q != slot)
                def _():
                    send(near, to_lr.at[q], from_lr, False, q).start()

        from_lr[slot] = to_lr[slot]

        @pl.loop(1, slots)
        def _(s):
            q = (slot + s) % slots
            arrival(near, to_lr.at[q], from_lr, False, q).wait_recv()

        if u == 0:

            @pl.loop(0, slots)
            def _(q):
                arrival(1, to_lr.at[q, 1], recv_far, True, q).wait_recv()

            @pl.loop(0, own)
            def _(c):
                for q in range(slots):
                    at = pl.ds(q * rows, rows)
                    left_f[at, :] = from_lr[q, 0, c].astype(F32)
                    right_f[side, at, :] = from_lr[q, 1, c].astype(F32)
                    right_f[1 - side, at, :] = recv_far[q, c].astype(F32)
                right = right_f[...].reshape(cols, cols).astype(BF16)
                prod_f[0] = lax.dot_general(
                    left_f[...].astype(BF16), right, NT, preferred_element_type=F32
                )
                for q in range(slots):
                    send_p[q, c] = prod_f[0, q * rows : (q + 1) * rows, :].astype(BF16)

            @pl.loop(1, slots)
            def _(s):
                q = (slot + s) % slots
                send(2, send_p.at[q], recv_p, False, q).start()

            recv_p[slot] = send_p[slot]

            @pl.loop(1, slots)
            def _(s):
                q = (slot + s) % slots
                arrival(2, send_p.at[q], recv_p, False, q).wait_recv()

        else:

            @pl.loop(0, own)
            def _(c):
                for q in range(slots):
                    at = pl.ds(q * rows, rows)
                    left_f[at, :] = from_lr[q, 0, c].astype(F32)
                    right_f[0, at, :] = from_lr[q, 1, c].astype(F32)
                prod_f[...] = lax.dot_general(
                    left_f[...].astype(BF16), right_f[0].astype(BF16), TN,
                    preferred_element_type=F32,
                ).reshape(2, cols // 2, cols)
                for e in range(2):
                    for q in range(slots):
                        send_q[e, q, c] = prod_f[e, q * rows : (q + 1) * rows, :].astype(BF16)

            @pl.loop(0, slots)
            def _(s):
                q = (slot + s) % slots
                send(5, send_q.at[1 - side, q], recv_q.at[1], True, q).start()

                @pl.when(q != slot)
                def _():
                    send(4, send_q.at[side, q], recv_q.at[0], False, q).start()

            recv_q[0, slot] = send_q[side, slot]

            @pl.loop(0, slots)
            def _(q):
                @pl.when(q != slot)
                def _():
                    arrival(4, send_q.at[side, q], recv_q.at[0], False, q).wait_recv()

                arrival(5, send_q.at[1 - side, q], recv_q.at[1], True, q).wait_recv()
                for c in range(own):
                    recv_p[q, c] = (
                        recv_q[0, q, c].astype(F32) + recv_q[1, q, c].astype(F32)
                    ).astype(BF16)

        def add(q, sums):
            total, squares = sums
            for c in range(own):
                v = recv_p[q, c].astype(F32)
                total, squares = total + v, squares + v * v
            return total, squares

        zero = jnp.zeros((rows, cols), F32)
        total, squares = lax.fori_loop(0, slots, add, (zero, zero))
        average = total / chans
        scale = lax.rsqrt(jnp.maximum(squares / chans - average * average, 0.0) + 1e-5)

        @pl.loop(0, slots)
        def _(q):
            for c in range(own):
                at = pl.multiple_of((q * own + c) * rows_pad, 8)
                piece = (recv_p[q, c].astype(F32) - average) * scale
                for t in range(cols // 128):
                    norm_f[t, pl.ds(at, rows), :] = piece[:, t * 128 : (t + 1) * 128]

        w_out = jnp.concatenate(
            [wfull[h, u, 4 * half : 5 * half] for h in range(cores)], axis=0
        )
        gain_out = jnp.concatenate(
            [wfull[h, u, 5 * half : 6 * half] for h in range(cores)], axis=0
        ).astype(F32)
        w_gate = gate_ref[u]

        @pl.loop(0, rows)
        def _(i):
            scaled = jnp.concatenate(
                [
                    (norm_f[t, pl.ds(i, chans, stride=rows_pad), :] * gain_out).astype(BF16)
                    for t in range(cols // 128)
                ],
                axis=1,
            )
            update = lax.dot_general(scaled, w_out, TN, preferred_element_type=F32)
            gate = jax.nn.sigmoid(jnp.dot(x[i], w_gate, preferred_element_type=F32))
            result = (z[i].astype(F32) + gate * update).astype(BF16)
            if u == 0:
                z[i] = result
            else:
                out_ref[i] = result

    @pl.loop(0, slots)
    def _(q):
        arrival(1, send_lr.at[0, q, 1], recv_far, True, q).wait_send()
        arrival(5, send_q.at[1 - side, q], recv_q.at[1], True, q).wait_send()

        @pl.when(q != slot)
        def _():
            arrival(0, send_lr.at[0, q], recv_lr.at[0], False, q).wait_send()
            arrival(2, send_p.at[q], recv_p, False, q).wait_send()
            arrival(3, send_lr.at[1, q], recv_lr.at[1], False, q).wait_send()
            arrival(4, send_q.at[side, q], recv_q.at[0], False, q).wait_send()


def shards(pair, seq_len, pair_mask, ln_in_gain, w_proj, w_gate, ln_out_gain, w_out):
    rows_chip, cols, feats = pair.shape
    cores = lax.axis_size("chan")
    slots = lax.axis_size("rows") * cores // 2
    rows = rows_chip // cores
    rows_pad = -(-rows // 8) * 8
    half = w_proj.shape[3]
    chans = half * cores
    own = chans // slots
    first = (lax.axis_index("rows") * cores + lax.axis_index("chan")) * rows
    valid = (jnp.arange(cols) < seq_len[0]).astype(F32)
    mask = lax.dynamic_slice_in_dim(pair_mask, lax.axis_index("chan") * rows, rows, 0)
    weight = (
        mask.astype(F32) * lax.dynamic_slice_in_dim(valid, first, rows)[:, None] * valid[None, :]
    )[:, None, :]
    pack = jnp.concatenate(
        [
            w_proj.transpose(0, 1, 3, 2).reshape(2, 4 * half, feats),
            w_out,
            jnp.broadcast_to(ln_out_gain[:, :, None], (2, half, feats)),
        ],
        axis=1,
    )
    dims = (slots, cores, rows, rows_pad, cols, chans, own, feats)
    tiles = cols // 128
    vmem = pl.BlockSpec(memory_space=pltpu.VMEM)
    return pl.pallas_call(
        functools.partial(kernel, dims),
        out_shape=jax.ShapeDtypeStruct((rows, cols, feats), BF16),
        in_specs=[pl.BlockSpec(memory_space=pl.ANY), vmem, vmem, vmem, vmem],
        out_specs=vmem,
        scratch_shapes=[
            pltpu.VMEM((rows, cols, feats), BF16),
            pltpu.VMEM((rows, cols, feats), BF16),
            pltpu.VMEM((cores,) + pack.shape, BF16),
            pltpu.VMEM((tiles, rows * 2 * half, 128), F32),
            pltpu.VMEM((cols // 2, cols), F32),
            pltpu.VMEM((2, cols // 2, cols), F32),
            pltpu.VMEM((2, cols // 2, cols), F32),
            pltpu.VMEM((tiles, chans * rows_pad, 128), F32),
            pltpu.VMEM((2, slots, 2, own, rows, cols), BF16),
            pltpu.VMEM((2, slots, 2, own, rows, cols), BF16),
            pltpu.VMEM((slots, own, rows, cols), BF16),
            pltpu.VMEM((slots, own, rows, cols), BF16),
            pltpu.VMEM((slots, own, rows, cols), BF16),
            pltpu.VMEM((2, slots, own, rows, cols), BF16),
            pltpu.VMEM((2, slots, own, rows, cols), BF16),
            pltpu.SemaphoreType.DMA((2,)),
            pltpu.SemaphoreType.DMA,
            pltpu.SemaphoreType.DMA,
            pltpu.SemaphoreType.DMA((6, slots)),
            pltpu.SemaphoreType.DMA((6, slots)),
        ],
        compiler_params=pltpu.CompilerParams(
            collective_id=0, has_side_effects=True, vmem_limit_bytes=60 * 1024 * 1024
        ),
        name="triangle",
    )(pair, weight, pack, ln_in_gain, w_gate)


def solution(mesh):
    in_specs = (
        P(("groups", "rows"), None, None),
        P("groups"),
        P(("groups", "rows"), None),
        P(),
        P(None, None, None, "chan"),
        P(),
        P(None, "chan"),
        P(None, "chan", None),
    )
    out_specs = P(("groups", "rows", "chan"), None, None)
    return jax.shard_map(shards, mesh=mesh, in_specs=in_specs, out_specs=out_specs, check_vma=False)
```

```python
import functools

import jax
import jax.numpy as jnp
from jax import lax
from jax.experimental import pallas as pl
from jax.experimental.pallas import tpu as pltpu
from jax.sharding import PartitionSpec as P

F32 = jnp.float32
BF16 = jnp.bfloat16
NT = (((1,), (1,)), ((), ()))
TN = (((0,), (0,)), ((), ()))


def kernel(
    dims, pair_ref, weight_ref, pack_ref, gain_ref, gate_ref, out_ref,
    z, x, gates, wfull, rows_f, left_f, right_f, prod_f, norm_f,
    send_lr, recv_lr, recv_far, send_p, recv_p, send_q, recv_q,
    local_sem, wsend_sem, wrecv_sem, send_sem, recv_sem, part_send, part_recv,
):
    slots, cores, rows, rows_pad, cols, chans, own, feats = dims
    peers = 2 * slots
    half = chans // cores
    slots_core = slots // cores
    part = 2
    parts = own // part
    core = lax.axis_index("chan")
    me = lax.axis_index("rows") * cores + core
    side = me // slots
    slot = me % slots

    def device(p):
        return {"rows": p // cores, "chan": p % cores}

    load = pltpu.make_async_copy(pair_ref.at[pl.ds(core * rows, rows)], z, local_sem.at[0])
    load.start()
    keep = pltpu.make_async_copy(pack_ref, wfull.at[core], local_sem.at[1])
    keep.start()

    barrier = pltpu.get_barrier_semaphore()

    @pl.loop(1, peers)
    def _(s):
        pl.semaphore_signal(
            barrier, inc=1, device_id=device((me + s) % peers), device_id_type=pl.DeviceIdType.MESH
        )

    pl.semaphore_wait(barrier, peers - 1)

    share = pltpu.make_async_remote_copy(
        src_ref=pack_ref, dst_ref=wfull.at[core], send_sem=wsend_sem, recv_sem=wrecv_sem,
        device_id=device(me - core + 1 - core), device_id_type=pl.DeviceIdType.MESH,
    )
    share.start()
    load.wait()

    def send(phase, src, dst, far, q):
        return pltpu.make_async_remote_copy(
            src_ref=src, dst_ref=dst.at[slot],
            send_sem=send_sem.at[phase, q], recv_sem=recv_sem.at[phase, slot],
            device_id=device((1 - side if far else side) * slots + q),
            device_id_type=pl.DeviceIdType.MESH,
        )

    def arrival(phase, src, dst, far, q):
        return pltpu.make_async_remote_copy(
            src_ref=src, dst_ref=dst.at[q],
            send_sem=send_sem.at[phase, q], recv_sem=recv_sem.at[phase, q],
            device_id=device((1 - side if far else side) * slots + q),
            device_id_type=pl.DeviceIdType.MESH,
        )

    def part_copy(phase, src, dst, far, q, g, to):
        at = pl.ds(g * part, part)
        if phase == 0:
            src, dst = src.at[:, at], dst.at[to, :, at]
        else:
            src, dst = src.at[at], dst.at[to, at]
        return pltpu.make_async_remote_copy(
            src_ref=src, dst_ref=dst,
            send_sem=part_send.at[phase, g, q], recv_sem=part_recv.at[phase, g, to],
            device_id=device((1 - side if far else side) * slots + q),
            device_id_type=pl.DeviceIdType.MESH,
        )

    def normalize_rows(u):
        gain_in = gain_ref[pl.ds(u, 1), :].astype(F32)

        @pl.loop(0, rows)
        def _(i):
            v = z[i].astype(F32)
            average = jnp.mean(v, axis=1, keepdims=True)
            squares = jnp.mean(v * v, axis=1, keepdims=True)
            spread = jnp.maximum(squares - average * average, 0.0)
            x[i] = ((v - average) * lax.rsqrt(spread + 1e-5) * gain_in).astype(BF16)

    def project(u, h):
        @pl.loop(0, rows)
        def _(i):
            w = weight_ref[i]
            p_t = lax.dot_general(wfull[h, u, : 4 * half], x[i], NT, preferred_element_type=F32)
            for lr in range(2):
                g = p_t[2 * lr * half : (2 * lr + 1) * half]
                val = p_t[(2 * lr + 1) * half : (2 * lr + 2) * half]
                at = pl.multiple_of(i * (2 * half) + lr * half, 8)
                piece = w * jax.nn.sigmoid(g) * val
                for t in range(cols // 128):
                    rows_f[t, pl.ds(at, half), :] = piece[:, t * 128 : (t + 1) * 128]

    def fill(q, target):
        for lr in range(2):
            for c in range(own):
                for t in range(cols // 128):
                    target[lr, c, :, t * 128 : (t + 1) * 128] = rows_f[
                        t, pl.ds(lr * half + q * own + c, rows, stride=2 * half), :
                    ].astype(BF16)

    for u in range(2):
        to_lr, from_lr = send_lr.at[u], recv_lr.at[u]
        normalize_rows(u)
        if u == 0:
            keep.wait()
            share.wait()

        for turn in range(cores):
            h = (slot // slots_core + 1 + turn) % cores
            project(u, h)

            @pl.loop(0, slots_core)
            def _(s):
                r = (slot + s) % slots_core
                q = h * slots_core + r
                fill(r, to_lr.at[q])
                if u == 0:
                    send(1, to_lr.at[q, 1], recv_far, True, q).start()

                    @pl.when(q != slot)
                    def _():
                        send(0, to_lr.at[q], from_lr, False, q).start()

            if u == 1:

                @pl.loop(0, parts)
                def _(g):
                    @pl.loop(0, slots_core)
                    def _(s):
                        q = h * slots_core + (slot + s) % slots_core

                        @pl.when(q != slot)
                        def _():
                            part_copy(0, to_lr.at[q], from_lr, False, q, g, slot).start()

        from_lr[slot] = to_lr[slot]
        w_gate = gate_ref[u]

        def open_gates(first, count):
            @pl.loop(0, count)
            def _(j):
                gates[first + j] = jax.nn.sigmoid(
                    jnp.dot(x[first + j], w_gate, preferred_element_type=F32)
                )

        if u == 0:
            open_gates(0, rows)

            @pl.loop(1, slots)
            def _(s):
                q = (slot + s) % slots
                arrival(0, to_lr.at[q], from_lr, False, q).wait_recv()

            @pl.loop(0, slots)
            def _(q):
                arrival(1, to_lr.at[q, 1], recv_far, True, q).wait_recv()

            @pl.loop(0, own)
            def _(c):
                for q in range(slots):
                    at = pl.ds(q * rows, rows)
                    left_f[at, :] = from_lr[q, 0, c].astype(F32)
                    right_f[side, at, :] = from_lr[q, 1, c].astype(F32)
                    right_f[1 - side, at, :] = recv_far[q, c].astype(F32)
                right = right_f[...].reshape(cols, cols).astype(BF16)
                prod_f[0] = lax.dot_general(
                    left_f[...].astype(BF16), right, NT, preferred_element_type=F32
                )
                for q in range(slots):
                    send_p[q, c] = prod_f[0, q * rows : (q + 1) * rows, :].astype(BF16)

            @pl.loop(1, slots)
            def _(s):
                q = (slot + s) % slots
                send(2, send_p.at[q], recv_p, False, q).start()

            recv_p[slot] = send_p[slot]

            @pl.loop(1, slots)
            def _(s):
                q = (slot + s) % slots
                arrival(2, send_p.at[q], recv_p, False, q).wait_recv()

        else:

            @pl.loop(0, parts)
            def _(g):
                @pl.loop(1, slots)
                def _(s):
                    q = (slot + s) % slots
                    part_copy(0, to_lr.at[q], from_lr, False, q, g, q).wait_recv()

                @pl.loop(0, part)
                def _(d):
                    c = g * part + d
                    for q in range(slots):
                        at = pl.ds(q * rows, rows)
                        left_f[at, :] = from_lr[q, 0, c].astype(F32)
                        right_f[0, at, :] = from_lr[q, 1, c].astype(F32)
                    prod_f[...] = lax.dot_general(
                        left_f[...].astype(BF16), right_f[0].astype(BF16), TN,
                        preferred_element_type=F32,
                    ).reshape(2, cols // 2, cols)
                    for e in range(2):
                        for q in range(slots):
                            send_q[e, q, c] = prod_f[e, q * rows : (q + 1) * rows, :].astype(BF16)

                @pl.loop(0, slots)
                def _(s):
                    q = (slot + s) % slots
                    part_copy(2, send_q.at[1 - side, q], recv_q.at[1], True, q, g, slot).start()

                    @pl.when(q != slot)
                    def _():
                        part_copy(1, send_q.at[side, q], recv_q.at[0], False, q, g, slot).start()

            recv_q[0, slot] = send_q[side, slot]
            open_gates(0, rows)

            @pl.loop(0, parts)
            def _(g):
                @pl.loop(0, slots)
                def _(q):
                    @pl.when(q != slot)
                    def _():
                        part_copy(1, send_q.at[side, q], recv_q.at[0], False, q, g, q).wait_recv()

                    part_copy(2, send_q.at[1 - side, q], recv_q.at[1], True, q, g, q).wait_recv()
                    for d in range(part):
                        c = g * part + d
                        recv_p[q, c] = (
                            recv_q[0, q, c].astype(F32) + recv_q[1, q, c].astype(F32)
                        ).astype(BF16)

        def add(q, sums):
            total, squares = sums
            for c in range(own):
                v = recv_p[q, c].astype(F32)
                total, squares = total + v, squares + v * v
            return total, squares

        zero = jnp.zeros((rows, cols), F32)
        total, squares = lax.fori_loop(0, slots, add, (zero, zero))
        average = total / chans
        scale = lax.rsqrt(jnp.maximum(squares / chans - average * average, 0.0) + 1e-5)

        @pl.loop(0, slots)
        def _(q):
            for c in range(own):
                at = pl.multiple_of((q * own + c) * rows_pad, 8)
                piece = (recv_p[q, c].astype(F32) - average) * scale
                for t in range(cols // 128):
                    norm_f[t, pl.ds(at, rows), :] = piece[:, t * 128 : (t + 1) * 128]

        w_out = jnp.concatenate(
            [wfull[h, u, 4 * half : 5 * half] for h in range(cores)], axis=0
        )
        gain_out = jnp.concatenate(
            [wfull[h, u, 5 * half : 6 * half] for h in range(cores)], axis=0
        ).astype(F32)

        @pl.loop(0, rows)
        def _(i):
            scaled = jnp.concatenate(
                [
                    (norm_f[t, pl.ds(i, chans, stride=rows_pad), :] * gain_out).astype(BF16)
                    for t in range(cols // 128)
                ],
                axis=1,
            )
            update = lax.dot_general(scaled, w_out, TN, preferred_element_type=F32)
            result = (z[i].astype(F32) + gates[i] * update).astype(BF16)
            if u == 0:
                z[i] = result
            else:
                out_ref[i] = result

    @pl.loop(0, slots)
    def _(q):
        arrival(1, send_lr.at[0, q, 1], recv_far, True, q).wait_send()

        @pl.when(q != slot)
        def _():
            arrival(0, send_lr.at[0, q], recv_lr.at[0], False, q).wait_send()
            arrival(2, send_p.at[q], recv_p, False, q).wait_send()

        @pl.loop(0, parts)
        def _(g):
            part_copy(2, send_q.at[1 - side, q], recv_q.at[1], True, q, g, q).wait_send()

            @pl.when(q != slot)
            def _():
                part_copy(0, send_lr.at[1, q], recv_lr.at[1], False, q, g, q).wait_send()
                part_copy(1, send_q.at[side, q], recv_q.at[0], False, q, g, q).wait_send()


def shards(pair, seq_len, pair_mask, ln_in_gain, w_proj, w_gate, ln_out_gain, w_out):
    rows_chip, cols, feats = pair.shape
    cores = lax.axis_size("chan")
    slots = lax.axis_size("rows") * cores // 2
    rows = rows_chip // cores
    rows_pad = -(-rows // 8) * 8
    half = w_proj.shape[3]
    chans = half * cores
    own = chans // slots
    first = (lax.axis_index("rows") * cores + lax.axis_index("chan")) * rows
    valid = (jnp.arange(cols) < seq_len[0]).astype(F32)
    mask = lax.dynamic_slice_in_dim(pair_mask, lax.axis_index("chan") * rows, rows, 0)
    weight = (
        mask.astype(F32) * lax.dynamic_slice_in_dim(valid, first, rows)[:, None] * valid[None, :]
    )[:, None, :]
    pack = jnp.concatenate(
        [
            w_proj.transpose(0, 1, 3, 2).reshape(2, 4 * half, feats),
            w_out,
            jnp.broadcast_to(ln_out_gain[:, :, None], (2, half, feats)),
        ],
        axis=1,
    )
    dims = (slots, cores, rows, rows_pad, cols, chans, own, feats)
    tiles = cols // 128
    vmem = pl.BlockSpec(memory_space=pltpu.VMEM)
    return pl.pallas_call(
        functools.partial(kernel, dims),
        out_shape=jax.ShapeDtypeStruct((rows, cols, feats), BF16),
        in_specs=[pl.BlockSpec(memory_space=pl.ANY), vmem, vmem, vmem, vmem],
        out_specs=vmem,
        scratch_shapes=[
            pltpu.VMEM((rows, cols, feats), BF16),
            pltpu.VMEM((rows, cols, feats), BF16),
            pltpu.VMEM((rows, cols, feats), F32),
            pltpu.VMEM((cores,) + pack.shape, BF16),
            pltpu.VMEM((tiles, rows * 2 * half, 128), F32),
            pltpu.VMEM((cols // 2, cols), F32),
            pltpu.VMEM((2, cols // 2, cols), F32),
            pltpu.VMEM((2, cols // 2, cols), F32),
            pltpu.VMEM((tiles, chans * rows_pad, 128), F32),
            pltpu.VMEM((2, slots, 2, own, rows, cols), BF16),
            pltpu.VMEM((2, slots, 2, own, rows, cols), BF16),
            pltpu.VMEM((slots, own, rows, cols), BF16),
            pltpu.VMEM((slots, own, rows, cols), BF16),
            pltpu.VMEM((slots, own, rows, cols), BF16),
            pltpu.VMEM((2, slots, own, rows, cols), BF16),
            pltpu.VMEM((2, slots, own, rows, cols), BF16),
            pltpu.SemaphoreType.DMA((2,)),
            pltpu.SemaphoreType.DMA,
            pltpu.SemaphoreType.DMA,
            pltpu.SemaphoreType.DMA((3, slots)),
            pltpu.SemaphoreType.DMA((3, slots)),
            pltpu.SemaphoreType.DMA((3, own // 2, slots)),
            pltpu.SemaphoreType.DMA((3, own // 2, slots)),
        ],
        compiler_params=pltpu.CompilerParams(
            collective_id=0, has_side_effects=True, vmem_limit_bytes=60 * 1024 * 1024
        ),
        name="triangle",
    )(pair, weight, pack, ln_in_gain, w_gate)


def solution(mesh):
    in_specs = (
        P(("groups", "rows"), None, None),
        P("groups"),
        P(("groups", "rows"), None),
        P(),
        P(None, None, None, "chan"),
        P(),
        P(None, "chan"),
        P(None, "chan", None),
    )
    out_specs = P(("groups", "rows", "chan"), None, None)
    return jax.shard_map(shards, mesh=mesh, in_specs=in_specs, out_specs=out_specs, check_vma=False)
```

```python
import functools

import jax
import jax.numpy as jnp
from jax import lax
from jax.experimental import pallas as pl
from jax.experimental.pallas import tpu as pltpu
from jax.sharding import PartitionSpec as P

F32 = jnp.float32
BF16 = jnp.bfloat16
NT = (((1,), (1,)), ((), ()))
TN = (((0,), (0,)), ((), ()))


def kernel(
    dims, pair_ref, weight_ref, pack_ref, gain_ref, gate_ref, out_ref,
    z, x, gates, wfull, rows_f, left_f, right_f, prod_f, norm_f,
    send_lr, recv_lr, recv_far, send_p, recv_p, send_q, recv_q,
    local_sem, wsend_sem, wrecv_sem, send_sem, recv_sem, part_send, part_recv,
):
    slots, cores, rows, rows_pad, cols, chans, own, feats = dims
    peers = 2 * slots
    half = chans // cores
    slots_core = slots // cores
    part = 2
    parts = own // part
    core = lax.axis_index("chan")
    me = lax.axis_index("rows") * cores + core
    side = me // slots
    slot = me % slots

    def device(p):
        return {"rows": p // cores, "chan": p % cores}

    load = pltpu.make_async_copy(pair_ref.at[pl.ds(core * rows, rows)], z, local_sem.at[0])
    load.start()
    keep = pltpu.make_async_copy(pack_ref, wfull.at[core], local_sem.at[1])
    keep.start()

    barrier = pltpu.get_barrier_semaphore()

    @pl.loop(1, peers)
    def _(s):
        pl.semaphore_signal(
            barrier, inc=1, device_id=device((me + s) % peers), device_id_type=pl.DeviceIdType.MESH
        )

    pl.semaphore_wait(barrier, peers - 1)

    share = pltpu.make_async_remote_copy(
        src_ref=pack_ref, dst_ref=wfull.at[core], send_sem=wsend_sem, recv_sem=wrecv_sem,
        device_id=device(me - core + 1 - core), device_id_type=pl.DeviceIdType.MESH,
    )
    share.start()
    load.wait()

    def send(phase, src, dst, far, q):
        return pltpu.make_async_remote_copy(
            src_ref=src, dst_ref=dst.at[slot],
            send_sem=send_sem.at[phase, q], recv_sem=recv_sem.at[phase, slot],
            device_id=device((1 - side if far else side) * slots + q),
            device_id_type=pl.DeviceIdType.MESH,
        )

    def arrival(phase, src, dst, far, q):
        return pltpu.make_async_remote_copy(
            src_ref=src, dst_ref=dst.at[q],
            send_sem=send_sem.at[phase, q], recv_sem=recv_sem.at[phase, q],
            device_id=device((1 - side if far else side) * slots + q),
            device_id_type=pl.DeviceIdType.MESH,
        )

    def part_copy(phase, src, dst, far, q, g, to):
        at = pl.ds(g * part, part)
        if phase == 0:
            src, dst = src.at[:, at], dst.at[to, :, at]
        else:
            src, dst = src.at[at], dst.at[to, at]
        return pltpu.make_async_remote_copy(
            src_ref=src, dst_ref=dst,
            send_sem=part_send.at[phase, g, q], recv_sem=part_recv.at[phase, g, to],
            device_id=device((1 - side if far else side) * slots + q),
            device_id_type=pl.DeviceIdType.MESH,
        )

    def normalize_rows(u):
        gain_in = gain_ref[pl.ds(u, 1), :].astype(F32)

        @pl.loop(0, rows, unroll=6)
        def _(i):
            v = z[i].astype(F32)
            average = jnp.mean(v, axis=1, keepdims=True)
            squares = jnp.mean(v * v, axis=1, keepdims=True)
            spread = jnp.maximum(squares - average * average, 0.0)
            x[i] = ((v - average) * lax.rsqrt(spread + 1e-5) * gain_in).astype(BF16)

    def project(u, h):
        @pl.loop(0, rows, unroll=6)
        def _(i):
            w = weight_ref[i]
            p_t = lax.dot_general(wfull[h, u, : 4 * half], x[i], NT, preferred_element_type=F32)
            for lr in range(2):
                g = p_t[2 * lr * half : (2 * lr + 1) * half]
                val = p_t[(2 * lr + 1) * half : (2 * lr + 2) * half]
                at = pl.multiple_of(i * (2 * half) + lr * half, 8)
                piece = w * jax.nn.sigmoid(g) * val
                for t in range(cols // 128):
                    rows_f[t, pl.ds(at, half), :] = piece[:, t * 128 : (t + 1) * 128]

    def fill(q, target):
        for lr in range(2):
            for c in range(own):
                for t in range(cols // 128):
                    target[lr, c, :, t * 128 : (t + 1) * 128] = rows_f[
                        t, pl.ds(lr * half + q * own + c, rows, stride=2 * half), :
                    ].astype(BF16)

    for u in range(2):
        to_lr, from_lr = send_lr.at[u], recv_lr.at[u]
        normalize_rows(u)
        if u == 0:
            keep.wait()
            share.wait()

        for turn in range(cores):
            h = (slot // slots_core + 1 + turn) % cores
            project(u, h)

            @pl.loop(0, slots_core)
            def _(s):
                r = (slot + s) % slots_core
                q = h * slots_core + r
                fill(r, to_lr.at[q])
                if u == 0:
                    send(1, to_lr.at[q, 1], recv_far, True, q).start()

                    @pl.when(q != slot)
                    def _():
                        send(0, to_lr.at[q], from_lr, False, q).start()

            if u == 1:

                @pl.loop(0, parts)
                def _(g):
                    @pl.loop(0, slots_core)
                    def _(s):
                        q = h * slots_core + (slot + s) % slots_core

                        @pl.when(q != slot)
                        def _():
                            part_copy(0, to_lr.at[q], from_lr, False, q, g, slot).start()

        from_lr[slot] = to_lr[slot]
        w_gate = gate_ref[u]

        def open_gates(first, count):
            @pl.loop(0, count, unroll=6)
            def _(j):
                gates[first + j] = jax.nn.sigmoid(
                    jnp.dot(x[first + j], w_gate, preferred_element_type=F32)
                )

        if u == 0:
            open_gates(0, rows)

            @pl.loop(1, slots)
            def _(s):
                q = (slot + s) % slots
                arrival(0, to_lr.at[q], from_lr, False, q).wait_recv()

            @pl.loop(0, slots)
            def _(q):
                arrival(1, to_lr.at[q, 1], recv_far, True, q).wait_recv()

            @pl.loop(0, own)
            def _(c):
                for q in range(slots):
                    at = pl.ds(q * rows, rows)
                    left_f[at, :] = from_lr[q, 0, c].astype(F32)
                    right_f[side, at, :] = from_lr[q, 1, c].astype(F32)
                    right_f[1 - side, at, :] = recv_far[q, c].astype(F32)
                right = right_f[...].reshape(cols, cols).astype(BF16)
                prod_f[0] = lax.dot_general(
                    left_f[...].astype(BF16), right, NT, preferred_element_type=F32
                )
                for q in range(slots):
                    send_p[q, c] = prod_f[0, q * rows : (q + 1) * rows, :].astype(BF16)

            @pl.loop(1, slots)
            def _(s):
                q = (slot + s) % slots
                send(2, send_p.at[q], recv_p, False, q).start()

            recv_p[slot] = send_p[slot]

            @pl.loop(1, slots)
            def _(s):
                q = (slot + s) % slots
                arrival(2, send_p.at[q], recv_p, False, q).wait_recv()

        else:

            @pl.loop(0, parts)
            def _(g):
                @pl.loop(1, slots)
                def _(s):
                    q = (slot + s) % slots
                    part_copy(0, to_lr.at[q], from_lr, False, q, g, q).wait_recv()

                @pl.loop(0, part)
                def _(d):
                    c = g * part + d
                    for q in range(slots):
                        at = pl.ds(q * rows, rows)
                        left_f[at, :] = from_lr[q, 0, c].astype(F32)
                        right_f[0, at, :] = from_lr[q, 1, c].astype(F32)
                    prod_f[...] = lax.dot_general(
                        left_f[...].astype(BF16), right_f[0].astype(BF16), TN,
                        preferred_element_type=F32,
                    ).reshape(2, cols // 2, cols)
                    for e in range(2):
                        for q in range(slots):
                            send_q[e, q, c] = prod_f[e, q * rows : (q + 1) * rows, :].astype(BF16)

                @pl.loop(0, slots)
                def _(s):
                    q = (slot + s) % slots
                    part_copy(2, send_q.at[1 - side, q], recv_q.at[1], True, q, g, slot).start()

                    @pl.when(q != slot)
                    def _():
                        part_copy(1, send_q.at[side, q], recv_q.at[0], False, q, g, slot).start()

            recv_q[0, slot] = send_q[side, slot]
            open_gates(0, rows)

            @pl.loop(0, parts)
            def _(g):
                @pl.loop(0, slots)
                def _(q):
                    @pl.when(q != slot)
                    def _():
                        part_copy(1, send_q.at[side, q], recv_q.at[0], False, q, g, q).wait_recv()

                    part_copy(2, send_q.at[1 - side, q], recv_q.at[1], True, q, g, q).wait_recv()
                    for d in range(part):
                        c = g * part + d
                        recv_p[q, c] = (
                            recv_q[0, q, c].astype(F32) + recv_q[1, q, c].astype(F32)
                        ).astype(BF16)

        def add(q, sums):
            total, squares = sums
            for c in range(own):
                v = recv_p[q, c].astype(F32)
                total, squares = total + v, squares + v * v
            return total, squares

        zero = jnp.zeros((rows, cols), F32)
        total, squares = lax.fori_loop(0, slots, add, (zero, zero), unroll=2)
        average = total / chans
        scale = lax.rsqrt(jnp.maximum(squares / chans - average * average, 0.0) + 1e-5)

        @pl.loop(0, slots, unroll=2)
        def _(q):
            for c in range(own):
                at = pl.multiple_of((q * own + c) * rows_pad, 8)
                piece = (recv_p[q, c].astype(F32) - average) * scale
                for t in range(cols // 128):
                    norm_f[t, pl.ds(at, rows), :] = piece[:, t * 128 : (t + 1) * 128]

        w_out = jnp.concatenate(
            [wfull[h, u, 4 * half : 5 * half] for h in range(cores)], axis=0
        )
        gain_out = jnp.concatenate(
            [wfull[h, u, 5 * half : 6 * half] for h in range(cores)], axis=0
        ).astype(F32)

        @pl.loop(0, rows, unroll=6)
        def _(i):
            scaled = jnp.concatenate(
                [
                    (norm_f[t, pl.ds(i, chans, stride=rows_pad), :] * gain_out).astype(BF16)
                    for t in range(cols // 128)
                ],
                axis=1,
            )
            update = lax.dot_general(scaled, w_out, TN, preferred_element_type=F32)
            result = (z[i].astype(F32) + gates[i] * update).astype(BF16)
            if u == 0:
                z[i] = result
            else:
                out_ref[i] = result

    @pl.loop(0, slots)
    def _(q):
        arrival(1, send_lr.at[0, q, 1], recv_far, True, q).wait_send()

        @pl.when(q != slot)
        def _():
            arrival(0, send_lr.at[0, q], recv_lr.at[0], False, q).wait_send()
            arrival(2, send_p.at[q], recv_p, False, q).wait_send()

        @pl.loop(0, parts)
        def _(g):
            part_copy(2, send_q.at[1 - side, q], recv_q.at[1], True, q, g, q).wait_send()

            @pl.when(q != slot)
            def _():
                part_copy(0, send_lr.at[1, q], recv_lr.at[1], False, q, g, q).wait_send()
                part_copy(1, send_q.at[side, q], recv_q.at[0], False, q, g, q).wait_send()


def shards(pair, seq_len, pair_mask, ln_in_gain, w_proj, w_gate, ln_out_gain, w_out):
    rows_chip, cols, feats = pair.shape
    cores = lax.axis_size("chan")
    slots = lax.axis_size("rows") * cores // 2
    rows = rows_chip // cores
    rows_pad = -(-rows // 8) * 8
    half = w_proj.shape[3]
    chans = half * cores
    own = chans // slots
    first = (lax.axis_index("rows") * cores + lax.axis_index("chan")) * rows
    valid = (jnp.arange(cols) < seq_len[0]).astype(F32)
    mask = lax.dynamic_slice_in_dim(pair_mask, lax.axis_index("chan") * rows, rows, 0)
    weight = (
        mask.astype(F32) * lax.dynamic_slice_in_dim(valid, first, rows)[:, None] * valid[None, :]
    )[:, None, :]
    pack = jnp.concatenate(
        [
            w_proj.transpose(0, 1, 3, 2).reshape(2, 4 * half, feats),
            w_out,
            jnp.broadcast_to(ln_out_gain[:, :, None], (2, half, feats)),
        ],
        axis=1,
    )
    dims = (slots, cores, rows, rows_pad, cols, chans, own, feats)
    tiles = cols // 128
    vmem = pl.BlockSpec(memory_space=pltpu.VMEM)
    return pl.pallas_call(
        functools.partial(kernel, dims),
        out_shape=jax.ShapeDtypeStruct((rows, cols, feats), BF16),
        in_specs=[pl.BlockSpec(memory_space=pl.ANY), vmem, vmem, vmem, vmem],
        out_specs=vmem,
        scratch_shapes=[
            pltpu.VMEM((rows, cols, feats), BF16),
            pltpu.VMEM((rows, cols, feats), BF16),
            pltpu.VMEM((rows, cols, feats), F32),
            pltpu.VMEM((cores,) + pack.shape, BF16),
            pltpu.VMEM((tiles, rows * 2 * half, 128), F32),
            pltpu.VMEM((cols // 2, cols), F32),
            pltpu.VMEM((2, cols // 2, cols), F32),
            pltpu.VMEM((2, cols // 2, cols), F32),
            pltpu.VMEM((tiles, chans * rows_pad, 128), F32),
            pltpu.VMEM((2, slots, 2, own, rows, cols), BF16),
            pltpu.VMEM((2, slots, 2, own, rows, cols), BF16),
            pltpu.VMEM((slots, own, rows, cols), BF16),
            pltpu.VMEM((slots, own, rows, cols), BF16),
            pltpu.VMEM((slots, own, rows, cols), BF16),
            pltpu.VMEM((2, slots, own, rows, cols), BF16),
            pltpu.VMEM((2, slots, own, rows, cols), BF16),
            pltpu.SemaphoreType.DMA((2,)),
            pltpu.SemaphoreType.DMA,
            pltpu.SemaphoreType.DMA,
            pltpu.SemaphoreType.DMA((3, slots)),
            pltpu.SemaphoreType.DMA((3, slots)),
            pltpu.SemaphoreType.DMA((3, own // 2, slots)),
            pltpu.SemaphoreType.DMA((3, own // 2, slots)),
        ],
        compiler_params=pltpu.CompilerParams(
            collective_id=0, has_side_effects=True, vmem_limit_bytes=60 * 1024 * 1024
        ),
        name="triangle",
    )(pair, weight, pack, ln_in_gain, w_gate)


def solution(mesh):
    in_specs = (
        P(("groups", "rows"), None, None),
        P("groups"),
        P(("groups", "rows"), None),
        P(),
        P(None, None, None, "chan"),
        P(),
        P(None, "chan"),
        P(None, "chan", None),
    )
    out_specs = P(("groups", "rows", "chan"), None, None)
    return jax.shard_map(shards, mesh=mesh, in_specs=in_specs, out_specs=out_specs, check_vma=False)
```

```python
import functools

import jax
import jax.numpy as jnp
from jax import lax
from jax.experimental import pallas as pl
from jax.experimental.pallas import tpu as pltpu
from jax.sharding import PartitionSpec as P

F32 = jnp.float32
BF16 = jnp.bfloat16
NT = (((1,), (1,)), ((), ()))
TN = (((0,), (0,)), ((), ()))


def kernel(
    dims, pair_ref, weight_ref, pack_ref, gain_ref, gate_ref, out_ref,
    z, x, gates, wfull, rows_f, left_f, right_f, prod_f, norm_f,
    send_lr, recv_lr, recv_far, send_p, recv_p, send_q, recv_q,
    local_sem, wsend_sem, wrecv_sem, send_sem, recv_sem, part_send, part_recv,
):
    slots, cores, rows, rows_pad, cols, chans, own, feats = dims
    peers = 2 * slots
    half = chans // cores
    slots_core = slots // cores
    part = 2
    parts = own // part
    core = lax.axis_index("chan")
    me = lax.axis_index("rows") * cores + core
    side = me // slots
    slot = me % slots

    def device(p):
        return {"rows": p // cores, "chan": p % cores}

    load = pltpu.make_async_copy(pair_ref.at[pl.ds(core * rows, rows)], z, local_sem.at[0])
    load.start()
    keep = pltpu.make_async_copy(pack_ref, wfull.at[core], local_sem.at[1])
    keep.start()

    barrier = pltpu.get_barrier_semaphore()

    @pl.loop(1, peers)
    def _(s):
        pl.semaphore_signal(
            barrier, inc=1, device_id=device((me + s) % peers), device_id_type=pl.DeviceIdType.MESH
        )

    pl.semaphore_wait(barrier, peers - 1)

    share = pltpu.make_async_remote_copy(
        src_ref=pack_ref, dst_ref=wfull.at[core], send_sem=wsend_sem, recv_sem=wrecv_sem,
        device_id=device(me - core + 1 - core), device_id_type=pl.DeviceIdType.MESH,
    )
    share.start()
    load.wait()

    def send(phase, src, dst, far, q):
        return pltpu.make_async_remote_copy(
            src_ref=src, dst_ref=dst.at[slot],
            send_sem=send_sem.at[phase, q], recv_sem=recv_sem.at[phase, slot],
            device_id=device((1 - side if far else side) * slots + q),
            device_id_type=pl.DeviceIdType.MESH,
        )

    def arrival(phase, src, dst, far, q):
        return pltpu.make_async_remote_copy(
            src_ref=src, dst_ref=dst.at[q],
            send_sem=send_sem.at[phase, q], recv_sem=recv_sem.at[phase, q],
            device_id=device((1 - side if far else side) * slots + q),
            device_id_type=pl.DeviceIdType.MESH,
        )

    def part_copy(phase, src, dst, far, q, g, to):
        at = pl.ds(g * part, part)
        if phase == 0:
            src, dst = src.at[:, at], dst.at[to, :, at]
        else:
            src, dst = src.at[at], dst.at[to, at]
        return pltpu.make_async_remote_copy(
            src_ref=src, dst_ref=dst,
            send_sem=part_send.at[phase, g, q], recv_sem=part_recv.at[phase, g, to],
            device_id=device((1 - side if far else side) * slots + q),
            device_id_type=pl.DeviceIdType.MESH,
        )

    def normalize_rows(u):
        gain_in = gain_ref[pl.ds(u, 1), :].astype(F32)

        @pl.loop(0, rows, unroll=(12 if rows % 12 == 0 else 6))
        def _(i):
            v = z[i].astype(F32)
            average = jnp.mean(v, axis=1, keepdims=True)
            squares = jnp.mean(v * v, axis=1, keepdims=True)
            spread = jnp.maximum(squares - average * average, 0.0)
            x[i] = ((v - average) * lax.rsqrt(spread + 1e-5) * gain_in).astype(BF16)

    def project(u, h):
        @pl.loop(0, rows, unroll=(12 if rows % 12 == 0 else 6))
        def _(i):
            w = weight_ref[i]
            p_t = lax.dot_general(wfull[h, u, : 4 * half], x[i], NT, preferred_element_type=F32)
            for lr in range(2):
                g = p_t[2 * lr * half : (2 * lr + 1) * half]
                val = p_t[(2 * lr + 1) * half : (2 * lr + 2) * half]
                at = pl.multiple_of(i * (2 * half) + lr * half, 8)
                piece = w * jax.nn.sigmoid(g) * val
                for t in range(cols // 128):
                    rows_f[t, pl.ds(at, half), :] = piece[:, t * 128 : (t + 1) * 128]

    def fill(q, target):
        for lr in range(2):
            for c in range(own):
                for t in range(cols // 128):
                    target[lr, c, :, t * 128 : (t + 1) * 128] = rows_f[
                        t, pl.ds(lr * half + q * own + c, rows, stride=2 * half), :
                    ].astype(BF16)

    for u in range(2):
        to_lr, from_lr = send_lr.at[u], recv_lr.at[u]
        normalize_rows(u)
        if u == 0:
            keep.wait()
            share.wait()

        for turn in range(cores):
            h = (slot // slots_core + 1 + turn) % cores
            project(u, h)

            @pl.loop(0, slots_core, unroll=2)
            def _(s):
                r = (slot + s) % slots_core
                q = h * slots_core + r
                fill(r, to_lr.at[q])
                if u == 0:
                    send(1, to_lr.at[q, 1], recv_far, True, q).start()

                    @pl.when(q != slot)
                    def _():
                        send(0, to_lr.at[q], from_lr, False, q).start()

            if u == 1:

                @pl.loop(0, parts)
                def _(g):
                    @pl.loop(0, slots_core)
                    def _(s):
                        q = h * slots_core + (slot + s) % slots_core

                        @pl.when(q != slot)
                        def _():
                            part_copy(0, to_lr.at[q], from_lr, False, q, g, slot).start()

        from_lr[slot] = to_lr[slot]
        w_gate = gate_ref[u]
        zero = jnp.zeros((rows, cols), F32)

        def open_gates(first, count):
            @pl.loop(0, count, unroll=(12 if rows % 12 == 0 else 6))
            def _(j):
                gates[first + j] = jax.nn.sigmoid(
                    jnp.dot(x[first + j], w_gate, preferred_element_type=F32)
                )

        if u == 0:
            open_gates(0, rows)

            @pl.loop(1, slots)
            def _(s):
                q = (slot + s) % slots
                arrival(0, to_lr.at[q], from_lr, False, q).wait_recv()

            @pl.loop(0, slots)
            def _(q):
                arrival(1, to_lr.at[q, 1], recv_far, True, q).wait_recv()

            @pl.loop(0, own, unroll=2)
            def _(c):
                for q in range(slots):
                    at = pl.ds(q * rows, rows)
                    left_f[at, :] = from_lr[q, 0, c].astype(F32)
                    right_f[side, at, :] = from_lr[q, 1, c].astype(F32)
                    right_f[1 - side, at, :] = recv_far[q, c].astype(F32)
                right = right_f[...].reshape(cols, cols).astype(BF16)
                prod_f[0] = lax.dot_general(
                    left_f[...].astype(BF16), right, NT, preferred_element_type=F32
                )
                for q in range(slots):
                    send_p[q, c] = prod_f[0, q * rows : (q + 1) * rows, :].astype(BF16)

            @pl.loop(1, slots)
            def _(s):
                q = (slot + s) % slots
                send(2, send_p.at[q], recv_p, False, q).start()

            recv_p[slot] = send_p[slot]

            @pl.loop(1, slots)
            def _(s):
                q = (slot + s) % slots
                arrival(2, send_p.at[q], recv_p, False, q).wait_recv()

            def add(q, sums):
                total, squares = sums
                for c in range(own):
                    v = recv_p[q, c].astype(F32)
                    total, squares = total + v, squares + v * v
                return total, squares

            total, squares = lax.fori_loop(0, slots, add, (zero, zero), unroll=2)

        else:

            @pl.loop(0, parts)
            def _(g):
                @pl.loop(1, slots)
                def _(s):
                    q = (slot + s) % slots
                    part_copy(0, to_lr.at[q], from_lr, False, q, g, q).wait_recv()

                @pl.loop(0, part, unroll=2)
                def _(d):
                    c = g * part + d
                    for q in range(slots):
                        at = pl.ds(q * rows, rows)
                        left_f[at, :] = from_lr[q, 0, c].astype(F32)
                        right_f[0, at, :] = from_lr[q, 1, c].astype(F32)
                    prod_f[...] = lax.dot_general(
                        left_f[...].astype(BF16), right_f[0].astype(BF16), TN,
                        preferred_element_type=F32,
                    ).reshape(2, cols // 2, cols)
                    for e in range(2):
                        for q in range(slots):
                            send_q[e, q, c] = prod_f[e, q * rows : (q + 1) * rows, :].astype(BF16)

                @pl.loop(0, slots)
                def _(s):
                    q = (slot + s) % slots
                    part_copy(2, send_q.at[1 - side, q], recv_q.at[1], True, q, g, slot).start()

                    @pl.when(q != slot)
                    def _():
                        part_copy(1, send_q.at[side, q], recv_q.at[0], False, q, g, slot).start()

            recv_q[0, slot] = send_q[side, slot]
            open_gates(0, rows)

            def take(step, sums):
                g, q = step // slots, step % slots

                @pl.when(q != slot)
                def _():
                    part_copy(1, send_q.at[side, q], recv_q.at[0], False, q, g, q).wait_recv()

                part_copy(2, send_q.at[1 - side, q], recv_q.at[1], True, q, g, q).wait_recv()
                total, squares = sums
                for d in range(part):
                    c = g * part + d
                    value = (
                        recv_q[0, q, c].astype(F32) + recv_q[1, q, c].astype(F32)
                    ).astype(BF16)
                    recv_p[q, c] = value
                    v = value.astype(F32)
                    total, squares = total + v, squares + v * v
                return total, squares

            total, squares = lax.fori_loop(0, parts * slots, take, (zero, zero))

        average = total / chans
        scale = lax.rsqrt(jnp.maximum(squares / chans - average * average, 0.0) + 1e-5)

        @pl.loop(0, slots, unroll=2)
        def _(q):
            for c in range(own):
                at = pl.multiple_of((q * own + c) * rows_pad, 8)
                piece = (recv_p[q, c].astype(F32) - average) * scale
                for t in range(cols // 128):
                    norm_f[t, pl.ds(at, rows), :] = piece[:, t * 128 : (t + 1) * 128]

        w_out = jnp.concatenate(
            [wfull[h, u, 4 * half : 5 * half] for h in range(cores)], axis=0
        )
        gain_out = jnp.concatenate(
            [wfull[h, u, 5 * half : 6 * half] for h in range(cores)], axis=0
        ).astype(F32)

        @pl.loop(0, rows, unroll=(12 if rows % 12 == 0 else 6))
        def _(i):
            scaled = jnp.concatenate(
                [
                    (norm_f[t, pl.ds(i, chans, stride=rows_pad), :] * gain_out).astype(BF16)
                    for t in range(cols // 128)
                ],
                axis=1,
            )
            update = lax.dot_general(scaled, w_out, TN, preferred_element_type=F32)
            result = (z[i].astype(F32) + gates[i] * update).astype(BF16)
            if u == 0:
                z[i] = result
            else:
                out_ref[i] = result

    @pl.loop(0, slots)
    def _(q):
        arrival(1, send_lr.at[0, q, 1], recv_far, True, q).wait_send()

        @pl.when(q != slot)
        def _():
            arrival(0, send_lr.at[0, q], recv_lr.at[0], False, q).wait_send()
            arrival(2, send_p.at[q], recv_p, False, q).wait_send()

        @pl.loop(0, parts)
        def _(g):
            part_copy(2, send_q.at[1 - side, q], recv_q.at[1], True, q, g, q).wait_send()

            @pl.when(q != slot)
            def _():
                part_copy(0, send_lr.at[1, q], recv_lr.at[1], False, q, g, q).wait_send()
                part_copy(1, send_q.at[side, q], recv_q.at[0], False, q, g, q).wait_send()


def shards(pair, seq_len, pair_mask, ln_in_gain, w_proj, w_gate, ln_out_gain, w_out):
    rows_chip, cols, feats = pair.shape
    cores = lax.axis_size("chan")
    slots = lax.axis_size("rows") * cores // 2
    rows = rows_chip // cores
    rows_pad = -(-rows // 8) * 8
    half = w_proj.shape[3]
    chans = half * cores
    own = chans // slots
    first = (lax.axis_index("rows") * cores + lax.axis_index("chan")) * rows
    valid = (jnp.arange(cols) < seq_len[0]).astype(F32)
    mask = lax.dynamic_slice_in_dim(pair_mask, lax.axis_index("chan") * rows, rows, 0)
    weight = (
        mask.astype(F32) * lax.dynamic_slice_in_dim(valid, first, rows)[:, None] * valid[None, :]
    )[:, None, :]
    pack = jnp.concatenate(
        [
            w_proj.transpose(0, 1, 3, 2).reshape(2, 4 * half, feats),
            w_out,
            jnp.broadcast_to(ln_out_gain[:, :, None], (2, half, feats)),
        ],
        axis=1,
    )
    dims = (slots, cores, rows, rows_pad, cols, chans, own, feats)
    tiles = cols // 128
    vmem = pl.BlockSpec(memory_space=pltpu.VMEM)
    return pl.pallas_call(
        functools.partial(kernel, dims),
        out_shape=jax.ShapeDtypeStruct((rows, cols, feats), BF16),
        in_specs=[pl.BlockSpec(memory_space=pl.ANY), vmem, vmem, vmem, vmem],
        out_specs=vmem,
        scratch_shapes=[
            pltpu.VMEM((rows, cols, feats), BF16),
            pltpu.VMEM((rows, cols, feats), BF16),
            pltpu.VMEM((rows, cols, feats), F32),
            pltpu.VMEM((cores,) + pack.shape, BF16),
            pltpu.VMEM((tiles, rows * 2 * half, 128), F32),
            pltpu.VMEM((cols // 2, cols), F32),
            pltpu.VMEM((2, cols // 2, cols), F32),
            pltpu.VMEM((2, cols // 2, cols), F32),
            pltpu.VMEM((tiles, chans * rows_pad, 128), F32),
            pltpu.VMEM((2, slots, 2, own, rows, cols), BF16),
            pltpu.VMEM((2, slots, 2, own, rows, cols), BF16),
            pltpu.VMEM((slots, own, rows, cols), BF16),
            pltpu.VMEM((slots, own, rows, cols), BF16),
            pltpu.VMEM((slots, own, rows, cols), BF16),
            pltpu.VMEM((2, slots, own, rows, cols), BF16),
            pltpu.VMEM((2, slots, own, rows, cols), BF16),
            pltpu.SemaphoreType.DMA((2,)),
            pltpu.SemaphoreType.DMA,
            pltpu.SemaphoreType.DMA,
            pltpu.SemaphoreType.DMA((3, slots)),
            pltpu.SemaphoreType.DMA((3, slots)),
            pltpu.SemaphoreType.DMA((3, own // 2, slots)),
            pltpu.SemaphoreType.DMA((3, own // 2, slots)),
        ],
        compiler_params=pltpu.CompilerParams(
            collective_id=0, has_side_effects=True, vmem_limit_bytes=60 * 1024 * 1024
        ),
        name="triangle",
    )(pair, weight, pack, ln_in_gain, w_gate)


def solution(mesh):
    in_specs = (
        P(("groups", "rows"), None, None),
        P("groups"),
        P(("groups", "rows"), None),
        P(),
        P(None, None, None, "chan"),
        P(),
        P(None, "chan"),
        P(None, "chan", None),
    )
    out_specs = P(("groups", "rows", "chan"), None, None)
    return jax.shard_map(shards, mesh=mesh, in_specs=in_specs, out_specs=out_specs, check_vma=False)
```
